256 devices in a mesh: outer: 64 (over y_lo, z, x), inner: 4 (over y_hi, core).
Axes of the slice: x: 4, y: 4 (y_hi: 2, y_lo: 2; y = y_hi * 2 + y_lo), z: 8, core: 2. Of those that a mesh axis runs over, the one named last changes fastest.
Arguments:
- frames: bfloat16 [32768, 1024], P(('outer', 'inner')), may hold values from -6 to 6
- gain_attn: float32 [1024], replicated, may hold values from 0.5 to 2
- w_query: bfloat16 [1024, 512], replicated, may hold values from -4 to 4
- w_key: bfloat16 [1024, 512], replicated, may hold values from -0.1875 to 0.1875
- w_value: bfloat16 [1024, 512], replicated, may hold values from -0.1875 to 0.1875
- w_out: bfloat16 [512, 1024], replicated, may hold values from -0.25 to 0.25
- gain_conv: float32 [1024], replicated, may hold values from 0.5 to 2
- w_expand: bfloat16 [1024, 2048], replicated, may hold values from -0.1875 to 0.1875
- kernel_taps: float32 [31, 1024], replicated, may hold values from -2 to 2
- bn_scale: float32 [1024], replicated, may hold values from 0.5 to 2
- bn_shift: float32 [1024], replicated, may hold values from -3 to 3
- w_project: bfloat16 [1024, 1024], replicated, may hold values from -0.1875 to 0.1875
Outputs:
- block_out: bfloat16 [32768, 1024], P(('outer', 'inner'))
The draws below stay inside these ranges and needn't reach their ends.
All inputs are finite; a program needn't handle non-finite values.
Results may differ from the reference program's by a relative error of at most 0.017.
The reference program's roundings to bfloat16 on the way (of `normed`, `context`, `hidden`, `normed2`, `glu` and `act`) count: a program that leaves them out, or rounds other values in their place, can miss the bound.
Values may be sent and summed in bfloat16 or wider, within the bound.
No kernel may reach another device: no remote copies, remote signals or barrier semaphores. Data moves between devices by JAX's collectives and lax.ppermute only.
A program may use at most 128 MiB of HBM per device.

```python
import math
import jax
import jax.numpy as jnp
from jax import lax

D = 1024
HEADS = 8
HEAD_DIM = 64
KERNEL = 31
SEQ = 32768


def draw_w_query(key, part):
    normal_draw = jax.random.normal(key, (D, HEADS * HEAD_DIM), jnp.float32)
    values = jnp.clip(normal_draw * 0.09, -4.0, 4.0)
    return values.astype(jnp.bfloat16)


def block_scale(rng, shape, split, least, largest):
    loudness, own = 1.0, jax.random.fold_in(rng, 6)
    for position, parts in split:
        draws = jnp.exp(jax.random.uniform(jax.random.fold_in(own, position), (parts,), jnp.float32, least / len(split), largest / len(split)))
        loudness = loudness * jnp.repeat(draws, shape[position] // parts).reshape([-1 if axis == position else 1 for axis in range(len(shape))])
    return loudness


def centred(stream_key, dims, scale, bound, cuts=(), held_as=jnp.bfloat16):
    level = block_scale(stream_key, dims, cuts, -0.22, 0.18) if cuts else 1.0
    drawn = jax.random.normal(stream_key, dims, jnp.float32) * scale * level
    return jnp.minimum(jnp.maximum(drawn, -bound), bound).astype(held_as)


def setup_inputs(seed: int = 0) -> dict:
    key_of = jax.random.split(jax.random.key(seed), 13)
    return {
        "frames": centred(key_of[0], (SEQ, D), 1.0, 6.0, ((0, 256),)),
        "gain_attn": jnp.clip(jnp.exp(jax.random.uniform(key_of[1], (D,), jnp.float32, math.log(0.5), math.log(2.0))), 0.5, 2.0),
        "w_query": draw_w_query(jax.random.fold_in(key_of[12], 71), 0),
        "w_key": centred(key_of[3], (D, HEADS * HEAD_DIM), D ** -0.5, 0.1875),
        "w_value": centred(key_of[4], (D, HEADS * HEAD_DIM), D ** -0.5, 0.1875),
        "w_out": centred(key_of[5], (HEADS * HEAD_DIM, D), (HEADS * HEAD_DIM) ** -0.5, 0.25),
        "gain_conv": jnp.clip(jnp.exp(jax.random.uniform(key_of[6], (D,), jnp.float32, math.log(0.5), math.log(2.0))), 0.5, 2.0),
        "w_expand": centred(key_of[7], (D, 2 * D), D ** -0.5, 0.1875),
        "kernel_taps": centred(key_of[8], (KERNEL, D), (KERNEL // 3) ** -0.5, 2.0, (), jnp.float32),
        "bn_scale": jnp.clip(jnp.exp(jax.random.uniform(key_of[9], (D,), jnp.float32, math.log(0.5), math.log(2.0))), 0.5, 2.0),
        "bn_shift": centred(key_of[10], (D,), 0.5, 3.0, (), jnp.float32),
        "w_project": centred(key_of[11], (D, D), D ** -0.5, 0.1875),
    }


def norm_rows(values, gain):
    values = values.astype(jnp.float32)
    center = values - lax.optimization_barrier(jnp.mean(values, axis=-1, keepdims=True))
    spread = lax.optimization_barrier(jnp.mean(center * center, axis=-1, keepdims=True))
    return center * lax.rsqrt(spread + 1e-05) * gain

def reference(frames, gain_attn, w_query, w_key, w_value, w_out, gain_conv, w_expand, kernel_taps, bn_scale, bn_shift, w_project):
    width = HEADS * HEAD_DIM
    normed = norm_rows(frames, gain_attn).astype(jnp.bfloat16)
    query = jnp.dot(normed, w_query, preferred_element_type=jnp.float32).astype(jnp.bfloat16)
    keys = jnp.dot(normed, w_key, preferred_element_type=jnp.float32).astype(jnp.bfloat16)
    values = jnp.dot(normed, w_value, preferred_element_type=jnp.float32).astype(jnp.bfloat16)
    scale = HEAD_DIM ** (-0.5)
    block = min(256, SEQ)
    query_blocks = query.reshape(SEQ // block, block, HEADS, HEAD_DIM)
    key_heads = keys.reshape(SEQ, HEADS, HEAD_DIM).astype(jnp.float32)
    value_heads = values.reshape(SEQ, HEADS, HEAD_DIM).astype(jnp.float32)

    def attend(query_block):
        scores = jnp.einsum('qhd,khd->hqk', query_block.astype(jnp.float32), key_heads) * scale
        top = lax.optimization_barrier(jnp.max(scores, axis=-1, keepdims=True))
        weights = jnp.exp(scores - top)
        total = lax.optimization_barrier(jnp.sum(weights, axis=-1))
        rounded = lax.optimization_barrier(weights.astype(jnp.bfloat16)).astype(jnp.float32)
        mixed = jnp.einsum('hqk,khd->qhd', rounded, value_heads)
        return mixed / jnp.transpose(total)[:, :, None]
    context = lax.map(attend, query_blocks).reshape(SEQ, width).astype(jnp.bfloat16)
    attn = jnp.dot(context, w_out, preferred_element_type=jnp.float32)
    hidden = (frames.astype(jnp.float32) + attn).astype(jnp.bfloat16)
    normed2 = norm_rows(hidden, gain_conv).astype(jnp.bfloat16)
    expand = jnp.dot(normed2, w_expand, preferred_element_type=jnp.float32)
    glu = (expand[:, :D] * jax.nn.sigmoid(expand[:, D:])).astype(jnp.bfloat16)
    half_kernel = KERNEL // 2
    padded = jnp.pad(glu.astype(jnp.float32), ((half_kernel, half_kernel), (0, 0)))
    conv = jnp.zeros((SEQ, D), jnp.float32)
    for tap in range(KERNEL):
        conv = conv + kernel_taps[tap] * padded[tap:tap + SEQ]
    act = jax.nn.silu(bn_scale * conv + bn_shift).astype(jnp.bfloat16)
    result = hidden.astype(jnp.float32) + jnp.dot(act, w_project, preferred_element_type=jnp.float32)
    return result.astype(jnp.bfloat16)
```

```python
import functools

import jax
import jax.numpy as jnp
from jax import lax
from jax.experimental import pallas as pl
from jax.experimental.pallas import tpu as pltpu
from jax.sharding import Mesh
from jax.sharding import PartitionSpec as P

BF = jnp.bfloat16
F32 = jnp.float32
D = 1024
HD = 64
OWN = 128
GRP = 1024
EPS = 1e-05
C = 0.125 * 1.4426950408889634
T_LOW, T_HIGH = 2.0 ** -60, 2.0 ** 100
TQ = 512
VMEM_LIMIT = 56 * 2 ** 20
NAMES = ("ylo", "z", "x", "yhi", "core")
YC = ("ylo", "yhi", "core")
VM = pl.BlockSpec(memory_space=pltpu.VMEM)
SM = pl.BlockSpec(memory_space=pltpu.SMEM)
ANY = pl.BlockSpec(memory_space=pl.ANY)


def call(kernel, ins, specs, outs, scratch=(), us=2):
    return pl.pallas_call(
        kernel,
        in_specs=specs,
        out_specs=[VM] * len(outs),
        out_shape=[jax.ShapeDtypeStruct(s, d) for s, d in outs],
        scratch_shapes=list(scratch),
        compiler_params=pltpu.CompilerParams(vmem_limit_bytes=VMEM_LIMIT),
        cost_estimate=pl.CostEstimate(flops=int(us * 1e9), bytes_accessed=1024, transcendentals=0),
    )(*ins)


def norm_rows(values, gain):
    values = values.astype(F32)
    center = values - jnp.mean(values, axis=-1, keepdims=True)
    spread = jnp.mean(center * center, axis=-1, keepdims=True)
    return center * lax.rsqrt(spread + EPS) * gain


def mm(a, b):
    return jnp.dot(a, b, preferred_element_type=F32)


def split3(row):
    hi = row.astype(BF)
    rest = row - hi.astype(F32)
    mid = rest.astype(BF)
    low = (rest - mid.astype(F32)).astype(BF)
    return hi, mid, low


def stats_rows(total, top):
    width = total.shape[1]
    index = lax.broadcasted_iota(jnp.int32, (16, width), 0)
    out = jnp.zeros((16, width), F32)
    for place, part in enumerate(split3(total) + split3(top)):
        out = jnp.where(index == place, jnp.broadcast_to(part.astype(F32), (16, width)), out)
    return out.astype(BF)


def stats_read(rows):
    rows = rows.astype(F32)
    return rows[0:1] + rows[1:2] + rows[2:3], rows[3:4] + rows[4:5] + rows[5:6]


def project_kernel(pos, own, sib, gain, wq, wk, wv, m0, m1, m2, m3, wbuf, sems):
    y, core = pos[0], pos[1]
    cols = pl.ds(pl.multiple_of(core * 256, 256), 256)
    copies = [
        pltpu.make_async_copy(w.at[:, cols], wbuf.at[i], sems.at[i]) for i, w in enumerate((wk, wv, wq))
    ]
    for copy in copies:
        copy.start()
    g = gain[...]
    normed = jnp.concatenate(
        [norm_rows(own[...], g).astype(BF), norm_rows(sib[...], g).astype(BF)], axis=0
    )
    copies[0].wait()
    k = mm(normed, wbuf[0])
    copies[1].wait()
    vt = mm(normed, wbuf[1]).T.astype(BF)
    copies[2].wait()
    qt = mm(normed, wbuf[2]).T.astype(BF)
    blocks = []
    for h in range(4):
        pair = jnp.concatenate([k[:OWN, h * HD:(h + 1) * HD], k[OWN:, h * HD:(h + 1) * HD]], axis=1).astype(BF)
        vh, qh = vt[h * HD:(h + 1) * HD], qt[h * HD:(h + 1) * HD]
        blocks.append(jnp.concatenate([pair, vh[:, :OWN], vh[:, OWN:], qh[:, :OWN], qh[:, OWN:]], axis=0))
    outs = (m0, m1, m2, m3)
    for here in range(4):
        @pl.when(y == here)
        def _():
            for i in range(4):
                outs[i][...] = blocks[(here + i) % 4]


def pair_and_values(kv, half):
    lhs = kv[0:512, :]
    cols = jnp.concatenate([kv[512 + half * 256 + i * 64:512 + half * 256 + (i + 1) * 64, :] for i in range(4)], axis=1)
    return lhs, jnp.concatenate([jnp.ones((64, 512), BF), cols], axis=0)


def place(q, half):
    zero = jnp.zeros((64, q.shape[1]), BF)
    return jnp.concatenate([q, zero] if half == 0 else [zero, q], axis=0)


def pack_kernel(a0, a1, a2, a3, kv, qx):
    parts = (a0, a1, a2, a3)
    for i, a in enumerate(parts):
        kv[i * 128:(i + 1) * 128, :] = a[0:128, :]
        kv[512 + i * 64:512 + (i + 1) * 64, :] = a[128:192, :]
        kv[768 + i * 64:768 + (i + 1) * 64, :] = a[192:256, :]
        qx[0:64, (2 * i) * 128:(2 * i + 1) * 128] = a[256:320, :]
        qx[0:64, (2 * i + 1) * 128:(2 * i + 2) * 128] = a[320:384, :]
    s = mm(kv[0:512, :], place(qx[0:64, :], 0))
    top = jnp.max(s, axis=0, keepdims=True)
    qx[64:80, :] = stats_rows(jnp.zeros_like(top), top)


def augmented(q, stats):
    unused, top = stats_read(stats)
    shift = top.astype(BF)
    width = shift.shape[1]
    index = lax.broadcasted_iota(jnp.int32, (128, width), 0)
    bias = jnp.where(index == 0, jnp.broadcast_to(-shift.astype(F32), (128, width)), 0.0).astype(BF)
    return [jnp.concatenate([place(q, half), bias], axis=0) for half in (0, 1)], shift.astype(F32)


def one_column(rows):
    lane = lax.broadcasted_iota(jnp.int32, (rows, 128), 1)
    return jnp.where(lane == 0, 1.0, 0.0).astype(BF)


def attend(rhs, chunks, acc):
    ones = one_column(512)

    def weights(step):
        kv, half = chunks[step // 2], step % 2
        lhs, values = pair_and_values(kv, half)
        s = mm(jnp.concatenate([lhs, ones], axis=1), rhs[half])
        return jnp.exp2(s * C).astype(BF), values

    steps = 2 * len(chunks)
    now = weights(0)
    for step in range(steps):
        later = weights(step + 1) if step + 1 < steps else None
        acc = acc + mm(now[1], now[0])
        now = later
    return acc


def exact(q_ref, chunks, kv_s, acc_ref, top_ref):
    for i, ref in enumerate(chunks):
        pltpu.sync_copy(ref, kv_s.at[i])

    def tile(t, carry):
        cols = pl.ds(pl.multiple_of(t * 256, 256), 256)
        q = q_ref[0:64, cols]

        def chunk(i, state):
            acc, old = state
            kv = kv_s.at[i]
            for half in (0, 1):
                lhs, values = pair_and_values(kv, half)
                s = mm(lhs, place(q, half))
                new = jnp.maximum(old, jnp.max(s, axis=0, keepdims=True))
                p = jnp.exp2((s - new) * C).astype(BF)
                acc = acc * jnp.exp2((old - new) * C) + mm(values, p)
                old = new
            return acc, old

        acc, top = lax.fori_loop(0, 8, chunk, (jnp.zeros((128, 256), F32), jnp.full((1, 256), -jnp.inf, F32)))
        acc_ref[:, cols] = acc
        top_ref[:, cols] = jnp.broadcast_to(top, (8, 256))
        return carry

    lax.fori_loop(0, q_ref.shape[1] // 256, tile, 0)


def finish(q_ref, chunks, kv_s, acc_ref, top_ref):
    total = acc_ref[0:1, :]
    fits = jnp.where((total >= T_LOW) & (total <= T_HIGH), 1.0, 0.0)

    @pl.when(jnp.min(fits) < 0.5)
    def _():
        exact(q_ref, chunks, kv_s, acc_ref, top_ref)


def tiles_of(q_ref, acc_in, chunks, acc_ref, top_ref):
    def tile(t, carry):
        cols = pl.ds(pl.multiple_of(t * TQ, TQ), TQ)
        rhs, shift = augmented(q_ref[0:64, cols], q_ref[64:80, cols])
        if acc_in is None:
            acc = jnp.zeros((128, TQ), F32)
        else:
            rows = acc_in[:, cols]
            acc = jnp.concatenate([jnp.broadcast_to(rows[0:1], (56, TQ)), rows], axis=0)
        acc = attend(rhs, chunks, acc)
        if top_ref is None:
            acc_ref[:, cols] = acc[56:128]
        else:
            acc_ref[:, cols] = acc
            top_ref[:, cols] = jnp.broadcast_to(shift, (8, TQ))
        return carry

    lax.fori_loop(0, q_ref.shape[1] // TQ, tile, 0)


def gather_queries(qs, q_s):
    for t in range(3):
        q_s[:, t * GRP:(t + 1) * GRP] = qs[t][...]


def start_kernel(qx, kv, acc):
    tiles_of(qx, None, [kv], acc, None)


def remote_kernel(count, first, last, *refs):
    refs = list(refs)
    qs, refs = refs[:3], refs[3:]
    chunks, refs = refs[:count], refs[count:]
    before, refs = (refs[:8 - count], refs[8 - count:]) if last else ([], refs)
    acc_in = None
    if not first:
        acc_in, refs = refs[0], refs[1:]
    if not last:
        acc, q_s = refs
        gather_queries(qs, q_s)
        tiles_of(q_s, acc_in, chunks, acc, None)
        return
    out0, out1, out2, q_s, acc_s, top_s, kv_s = refs
    gather_queries(qs, q_s)
    tiles_of(q_s, acc_in, chunks, acc_s, top_s)
    finish(q_s, before + chunks, kv_s, acc_s, top_s)
    for t, out in enumerate((out0, out1, out2)):
        cols = slice(t * GRP, (t + 1) * GRP)
        out[0:64, :] = acc_s[64:128, cols].astype(BF)
        out[64:80, :] = stats_rows(acc_s[0:1, cols], top_s[0:1, cols])


def own_kernel(count, *refs):
    qx, own_kv = refs[0], refs[1]
    chunks = list(refs[2:2 + count])
    acc_in, out, acc_s, top_s, kv_s = refs[2 + count:]
    tiles_of(qx, acc_in, chunks, acc_s, top_s)
    finish(qx, [own_kv] + chunks, kv_s, acc_s, top_s)
    out[0:64, :] = acc_s[64:128, :]
    out[64:72, :] = jnp.broadcast_to(acc_s[0:1, :], (8, GRP))
    out[72:80, :] = top_s[...]


def combine_kernel(pos, own, r1, r2, r3, out):
    y, core = pos[0], pos[1]
    sums = [own[0:64, :]] + [r[0:64, :].astype(F32) for r in (r1, r2, r3)]
    stats = [(own[64:65, :], own[72:73, :])] + [stats_read(r[64:80, :]) for r in (r1, r2, r3)]
    top = functools.reduce(jnp.maximum, [s[1] for s in stats])
    factors = [jnp.exp2((s[1] - top) * C) for s in stats]
    total = sum(f * s[0] for f, s in zip(factors, stats))
    context = (sum(f * s for f, s in zip(factors, sums)) / total).astype(BF)
    for i in range(4):
        to_y = lax.rem(y + 4 - i, 4)
        for j in range(2):
            to_core = core if j == 0 else 1 - core
            to = lax.rem(to_y, 2) * 4 + lax.div(to_y, 2) * 2 + to_core
            out[to] = context[:, (2 * i + j) * 128:(2 * i + j + 1) * 128]


def expand_kernel(ctx, frames, w_out, gain, w_expand, hidden, glu, head, tail, wo, we, sems):
    copies = [pltpu.make_async_copy(w_out, wo, sems.at[0])]
    for i in range(4):
        block = i % 2 * 1024 + i // 2 * 512
        copies.append(pltpu.make_async_copy(
            w_expand.at[:, block:block + 512], we.at[:, block:block + 512], sems.at[1 + i]))
    for copy in copies:
        copy.start()
    order = [yy % 2 * 4 + yy // 2 * 2 + cc for cc in range(2) for yy in range(4)]
    context = jnp.concatenate([ctx[s] for s in order], axis=0).T
    copies[0].wait()
    h = (frames[...].astype(F32) + mm(context, wo[...])).astype(BF)
    hidden[...] = h
    normed = norm_rows(h, gain[...]).astype(BF)
    for i in range(2):
        copies[1 + 2 * i].wait()
        value = mm(normed, we[:, i * 512:(i + 1) * 512])
        copies[2 + 2 * i].wait()
        gate = mm(normed, we[:, 1024 + i * 512:1024 + (i + 1) * 512])
        g = (value * jax.nn.sigmoid(gate)).astype(BF)
        cols = slice(i * 512, (i + 1) * 512)
        glu[:, cols] = g
        head[:, cols] = g[:16]
        tail[:, cols] = g[OWN - 16:]


def conv_kernel(before, glu, after, hidden, taps, scale, shift, w_project, out, pad, act, wp, sem):
    copy = pltpu.make_async_copy(w_project, wp, sem)
    copy.start()
    pad[0:16, :] = before[...].astype(F32)
    pad[16:16 + OWN, :] = glu[...].astype(F32)
    pad[16 + OWN:32 + OWN, :] = after[...].astype(F32)

    def block(i, carry):
        cols = pl.ds(pl.multiple_of(i * 128, 128), 128)
        conv = jnp.zeros((OWN, 128), F32)
        for tap in range(31):
            conv = conv + taps[tap:tap + 1, cols] * pad[1 + tap:1 + tap + OWN, cols]
        act[:, cols] = jax.nn.silu(scale[:, cols] * conv + shift[:, cols]).astype(BF)
        return carry

    lax.fori_loop(0, D // 128, block, 0)
    copy.wait()
    out[...] = (hidden[...].astype(F32) + mm(act[...], wp[...])).astype(BF)


def body(frames, gain_attn, w_query, w_key, w_value, w_out, gain_conv, w_expand, kernel_taps, bn_scale, bn_shift, w_project):
    core = lax.axis_index("core")
    y = lax.axis_index("yhi") * 2 + lax.axis_index("ylo")
    pos = jnp.stack([y, core]).astype(jnp.int32)

    def along(axis, value, step):
        count = lax.axis_size(axis)
        return lax.ppermute(value, axis, [(i, (i + step) % count) for i in range(count)])

    def along_y(value, step):
        place_of = lambda v: v % 2 * 2 + v // 2
        return lax.ppermute(value, ("ylo", "yhi"), [(place_of(i), place_of((i + step) % 4)) for i in range(4)])

    row = lambda v: v.reshape(1, -1)
    sib = along("core", frames, 1)
    sent = call(
        project_kernel, (pos, frames, sib, row(gain_attn), w_query, w_key, w_value), [SM, VM, VM, VM, ANY, ANY, ANY],
        [((384, 128), BF)] * 4, [pltpu.VMEM((3, D, 256), BF), pltpu.SemaphoreType.DMA((3,))],
    )
    got = [sent[0]] + [along_y(sent[i], i) for i in (1, 2, 3)]
    kv, qx = call(pack_kernel, got, [VM] * 4, [((GRP, 128), BF), ((80, GRP), BF)])
    up1, down1 = along("z", kv, 1), along("z", kv, -1)
    queries = [along("x", qx, i) for i in (1, 2, 3)]
    own_acc, = call(start_kernel, (qx, kv), [VM] * 2, [((72, GRP), F32)], us=2)
    up1, down1, own_acc = lax.optimization_barrier((up1, down1, own_acc))
    up2, down2 = along("z", up1, 1), along("z", down1, -1)
    many = ((72, 3 * GRP), F32)
    q_scratch = pltpu.VMEM((80, 3 * GRP), BF)
    acc, = call(
        functools.partial(remote_kernel, 3, True, False), (*queries, kv, up1, down1), [VM] * 6, [many], [q_scratch], us=10,
    )
    up2, down2, acc = lax.optimization_barrier((up2, down2, acc))
    up3, down3 = along("z", up2, 1), along("z", down2, -1)
    acc, = call(
        functools.partial(remote_kernel, 2, False, False), (*queries, up2, down2, acc), [VM] * 6, [many], [q_scratch], us=7,
    )
    up3, down3, acc = lax.optimization_barrier((up3, down3, acc))
    up4 = along("z", up3, 1)
    acc, = call(
        functools.partial(remote_kernel, 2, False, False), (*queries, up3, down3, acc), [VM] * 6, [many], [q_scratch], us=7,
    )
    parts = call(
        functools.partial(remote_kernel, 1, False, True),
        (*queries, up4, kv, up1, down1, up2, down2, up3, down3, acc), [VM] * 4 + [ANY] * 7 + [VM],
        [((80, GRP), BF)] * 3,
        [q_scratch, pltpu.VMEM((128, 3 * GRP), F32), pltpu.VMEM((8, 3 * GRP), F32), pltpu.VMEM((8, GRP, 128), BF)],
        us=4,
    )
    returned = [along("x", parts[i - 1], -i) for i in (1, 2, 3)]
    chunks = (up1, down1, up2, down2, up3, down3, up4)
    own_part, = call(
        functools.partial(own_kernel, 7), (qx, kv, *chunks, own_acc), [VM] * 10, [((80, GRP), F32)],
        [pltpu.VMEM((128, GRP), F32), pltpu.VMEM((8, GRP), F32), pltpu.VMEM((8, GRP, 128), BF)], us=8,
    )
    contexts, = call(combine_kernel, (pos, own_part, *returned), [SM] + [VM] * 4, [((8, HD, 128), BF)])
    contexts = lax.all_to_all(contexts, YC, 0, 0)
    hidden, glu, head, tail = call(
        expand_kernel, (contexts, frames, w_out, row(gain_conv), w_expand), [VM, VM, ANY, VM, ANY],
        [((OWN, D), BF), ((OWN, D), BF), ((16, D), BF), ((16, D), BF)],
        [pltpu.VMEM((512, D), BF), pltpu.VMEM((D, 2 * D), BF), pltpu.SemaphoreType.DMA((5,))],
    )
    count = lax.axis_size(NAMES)
    before = lax.ppermute(tail, NAMES, [(i, i + 1) for i in range(count - 1)])
    after = lax.ppermute(head, NAMES, [(i + 1, i) for i in range(count - 1)])
    out, = call(
        conv_kernel, (before, glu, after, hidden, kernel_taps, row(bn_scale), row(bn_shift), w_project),
        [VM] * 7 + [ANY], [((OWN, D), BF)],
        [pltpu.VMEM((OWN + 32, D), F32), pltpu.VMEM((OWN, D), BF), pltpu.VMEM((D, D), BF), pltpu.SemaphoreType.DMA],
    )
    return out


def solution(mesh):
    fine = Mesh(mesh.devices.reshape(2, 8, 4, 2, 2), NAMES)
    rows = P(NAMES, None)
    return jax.shard_map(
        body, mesh=fine, in_specs=(rows,) + (P(),) * 11, out_specs=rows, check_vma=False,
    )
```

```python
import functools

import jax
import jax.numpy as jnp
from jax import lax
from jax.experimental import pallas as pl
from jax.experimental.pallas import tpu as pltpu
from jax.sharding import Mesh
from jax.sharding import PartitionSpec as P

BF = jnp.bfloat16
F32 = jnp.float32
D = 1024
HD = 64
OWN = 128
GRP = 1024
EPS = 1e-05
C = 0.125 * 1.4426950408889634
T_LOW, T_HIGH = 2.0 ** -60, 2.0 ** 100
TQ = 1024
VMEM_LIMIT = 24 * 2 ** 20
NAMES = ("ylo", "z", "x", "yhi", "core")
VM = pl.BlockSpec(memory_space=pltpu.VMEM)
SM = pl.BlockSpec(memory_space=pltpu.SMEM)
ANY = pl.BlockSpec(memory_space=pl.ANY)
HBM = pl.BlockSpec(memory_space=pltpu.HBM)


def call(kernel, ins, specs, outs, scratch=(), us=2):
    return pl.pallas_call(
        kernel,
        in_specs=specs,
        out_specs=[VM] * len(outs),
        out_shape=[jax.ShapeDtypeStruct(s, d) for s, d in outs],
        scratch_shapes=list(scratch),
        compiler_params=pltpu.CompilerParams(vmem_limit_bytes=VMEM_LIMIT),
        cost_estimate=pl.CostEstimate(flops=int(us * 1e9), bytes_accessed=1024, transcendentals=0),
    )(*ins)


def norm_rows(values, gain):
    values = values.astype(F32)
    center = values - jnp.mean(values, axis=-1, keepdims=True)
    spread = jnp.mean(center * center, axis=-1, keepdims=True)
    return center * lax.rsqrt(spread + EPS) * gain


def mm(a, b):
    return jnp.dot(a, b, preferred_element_type=F32)


def split3(row):
    hi = row.astype(BF)
    rest = row - hi.astype(F32)
    mid = rest.astype(BF)
    low = (rest - mid.astype(F32)).astype(BF)
    return hi, mid, low


def stats_rows(total, top):
    width = total.shape[1]
    index = lax.broadcasted_iota(jnp.int32, (16, width), 0)
    out = jnp.zeros((16, width), F32)
    for place, part in enumerate(split3(total) + split3(top)):
        out = jnp.where(index == place, jnp.broadcast_to(part.astype(F32), (16, width)), out)
    return out.astype(BF)


def stats_read(rows):
    rows = rows.astype(F32)
    return rows[0:1] + rows[1:2] + rows[2:3], rows[3:4] + rows[4:5] + rows[5:6]


def project_kernel(pos, own_hbm, sib, gain_hbm, wq, wk, wv, m0, m1, m2, m3, own, gain, wbuf, sems):
    y, core = pos[0], pos[1]
    cols = pl.ds(pl.multiple_of(core * 256, 256), 256)
    first = [pltpu.make_async_copy(own_hbm, own, sems.at[3]), pltpu.make_async_copy(gain_hbm, gain, sems.at[4])]
    copies = [
        pltpu.make_async_copy(w.at[:, cols], wbuf.at[i], sems.at[i]) for i, w in enumerate((wk, wv, wq))
    ]
    for copy in first + copies:
        copy.start()
    for copy in first:
        copy.wait()
    g = gain[...]
    normed = jnp.concatenate(
        [norm_rows(own[...], g).astype(BF), norm_rows(sib[...], g).astype(BF)], axis=0
    )
    copies[0].wait()
    k = mm(normed, wbuf[0])
    copies[1].wait()
    vt = mm(normed, wbuf[1]).T.astype(BF)
    copies[2].wait()
    qt = mm(normed, wbuf[2]).T.astype(BF)
    blocks = []
    for h in range(4):
        pair = jnp.concatenate([k[:OWN, h * HD:(h + 1) * HD], k[OWN:, h * HD:(h + 1) * HD]], axis=1).astype(BF)
        vh, qh = vt[h * HD:(h + 1) * HD], qt[h * HD:(h + 1) * HD]
        blocks.append(jnp.concatenate([pair, vh[:, :OWN], vh[:, OWN:], qh[:, :OWN], qh[:, OWN:]], axis=0))
    outs = (m0, m1, m2, m3)
    for here in range(4):
        @pl.when(y == here)
        def _():
            for i in range(4):
                outs[i][...] = blocks[(here + i) % 4]


def pair_and_values(kv, half):
    lhs = kv[0:512, :]
    cols = jnp.concatenate([kv[512 + half * 256 + i * 64:512 + half * 256 + (i + 1) * 64, :] for i in range(4)], axis=1)
    return lhs, jnp.concatenate([jnp.ones((64, 512), BF), cols], axis=0)


def place(q, half):
    zero = jnp.zeros((64, q.shape[1]), BF)
    return jnp.concatenate([q, zero] if half == 0 else [zero, q], axis=0)


def pack_kernel(a0, a1, a2, a3, kv, qx):
    parts = (a0, a1, a2, a3)
    for i, a in enumerate(parts):
        kv[i * 128:(i + 1) * 128, :] = a[0:128, :]
        kv[512 + i * 64:512 + (i + 1) * 64, :] = a[128:192, :]
        kv[768 + i * 64:768 + (i + 1) * 64, :] = a[192:256, :]
        qx[0:64, (2 * i) * 128:(2 * i + 1) * 128] = a[256:320, :]
        qx[0:64, (2 * i + 1) * 128:(2 * i + 2) * 128] = a[320:384, :]
    s = mm(kv[0:512, :], place(qx[0:64, :], 0))
    top = jnp.max(s, axis=0, keepdims=True)
    qx[64:80, :] = stats_rows(jnp.zeros_like(top), top)


def augmented(q, stats):
    unused, top = stats_read(stats)
    shift = top.astype(BF)
    width = shift.shape[1]
    index = lax.broadcasted_iota(jnp.int32, (128, width), 0)
    bias = jnp.where(index == 0, jnp.broadcast_to(-shift.astype(F32), (128, width)), 0.0).astype(BF)
    return [jnp.concatenate([place(q, half), bias], axis=0) for half in (0, 1)], shift.astype(F32)


def one_column(rows):
    lane = lax.broadcasted_iota(jnp.int32, (rows, 128), 1)
    return jnp.where(lane == 0, 1.0, 0.0).astype(BF)


def attend(rhs, chunks, acc):
    ones = one_column(512)

    def weights(step):
        kv, half = chunks[step // 2], step % 2
        lhs, values = pair_and_values(kv, half)
        s = mm(jnp.concatenate([lhs, ones], axis=1), rhs[half])
        return jnp.exp2(s * C).astype(BF), values

    steps = 2 * len(chunks)
    now = weights(0)
    for step in range(steps):
        later = weights(step + 1) if step + 1 < steps else None
        acc = acc + mm(now[1], now[0])
        now = later
    return acc


def exact(q_ref, chunks, kv_s, acc_ref, top_ref, start):
    for i, ref in enumerate(chunks):
        pltpu.sync_copy(ref, kv_s.at[i])

    def tile(t, carry):
        cols = pl.ds(pl.multiple_of(t * 256, 256), 256)
        q = q_ref[0:64, pl.ds(pl.multiple_of(start + t * 256, 256), 256)]

        def chunk(i, state):
            acc, old = state
            kv = kv_s.at[i]
            for half in (0, 1):
                lhs, values = pair_and_values(kv, half)
                s = mm(lhs, place(q, half))
                new = jnp.maximum(old, jnp.max(s, axis=0, keepdims=True))
                p = jnp.exp2((s - new) * C).astype(BF)
                acc = acc * jnp.exp2((old - new) * C) + mm(values, p)
                old = new
            return acc, old

        acc, top = lax.fori_loop(0, 8, chunk, (jnp.zeros((128, 256), F32), jnp.full((1, 256), -jnp.inf, F32)))
        acc_ref[:, cols] = acc
        top_ref[:, cols] = jnp.broadcast_to(top, (8, 256))
        return carry

    lax.fori_loop(0, acc_ref.shape[1] // 256, tile, 0)


def finish(q_ref, chunks, kv_s, acc_ref, top_ref, start=0):
    total = acc_ref[0:1, :]
    fits = jnp.where((total >= T_LOW) & (total <= T_HIGH), 1.0, 0.0)

    @pl.when(jnp.min(fits) < 0.5)
    def _():
        exact(q_ref, chunks, kv_s, acc_ref, top_ref, start)


def tiles_of(q_ref, acc_in, chunks, acc_ref, top_ref, start=0, size=TQ, count=None):
    def tile(t, carry):
        from_cols = pl.ds(pl.multiple_of(start + t * size, 256), size)
        cols = pl.ds(pl.multiple_of(t * size, 256), size)
        rhs, shift = augmented(q_ref[0:64, from_cols], q_ref[64:80, from_cols])
        if acc_in is None:
            acc = jnp.zeros((128, size), F32)
        else:
            rows = acc_in[:, from_cols]
            acc = jnp.concatenate([jnp.broadcast_to(rows[0:1], (56, size)), rows], axis=0)
        acc = attend(rhs, chunks, acc)
        if top_ref is None:
            acc_ref[:, cols] = acc[56:128]
        else:
            acc_ref[:, cols] = acc
            top_ref[:, cols] = jnp.broadcast_to(shift, (8, size))
        return carry

    lax.fori_loop(0, q_ref.shape[1] // size if count is None else count, tile, 0)


def gather_queries(qs, q_s):
    for t in range(3):
        q_s[:, t * GRP:(t + 1) * GRP] = qs[t][...]


def start_kernel(qx, kv, acc):
    tiles_of(qx, None, [kv], acc, None)


def remote_kernel(count, first, last, *refs):
    refs = list(refs)
    qs, refs = refs[:3], refs[3:]
    chunks, refs = refs[:count], refs[count:]
    before, refs = (refs[:8 - count], refs[8 - count:]) if last else ([], refs)
    acc_in = None
    if not first:
        acc_in, refs = refs[0], refs[1:]
    if not last:
        acc, q_s = refs
        gather_queries(qs, q_s)
        tiles_of(q_s, acc_in, chunks, acc, None)
        return
    out0, out1, out2, q_s, acc_s, top_s, kv_s = refs
    gather_queries(qs, q_s)
    tiles_of(q_s, acc_in, chunks, acc_s, top_s)
    finish(q_s, before + chunks, kv_s, acc_s, top_s)
    for t, out in enumerate((out0, out1, out2)):
        cols = slice(t * GRP, (t + 1) * GRP)
        out[0:64, :] = acc_s[64:128, cols].astype(BF)
        out[64:80, :] = stats_rows(acc_s[0:1, cols], top_s[0:1, cols])


def own_sums(qx, own_kv, chunks, acc_in, acc_s, top_s, kv_s, start, size):
    tiles_of(qx, acc_in, chunks, acc_s, top_s, start, size, 1)
    finish(qx, [own_kv] + chunks, kv_s, acc_s, top_s, start)


def others_kernel(count, *refs):
    acc_in, out, acc_s, top_s, kv_s = refs[2 + count:]
    own_sums(refs[0], refs[1], list(refs[2:2 + count]), acc_in, acc_s, top_s, kv_s, 256, 768)
    out[0:64, :] = acc_s[64:128, :]
    out[64:72, :] = jnp.broadcast_to(acc_s[0:1, :], (8, 768))
    out[72:80, :] = top_s[...]


def context_of(sums, total, top, received, cols):
    sums = [sums] + [r[0:64, cols].astype(F32) for r in received]
    stats = [(total, top)] + [stats_read(r[64:80, cols]) for r in received]
    top = functools.reduce(jnp.maximum, [s[1] for s in stats])
    factors = [jnp.exp2((s[1] - top) * C) for s in stats]
    total = sum(f * s[0] for f, s in zip(factors, stats))
    return (sum(f * s for f, s in zip(factors, sums)) / total).astype(BF)


def combine_kernel(part, r1, r2, r3, c1, c2, c3):
    context = context_of(part[0:64, :], part[64:65, :], part[72:73, :], (r1, r2, r3), slice(256, 1024))
    for i, out in enumerate((c1, c2, c3)):
        out[0:64, :] = context[:, i * 256:i * 256 + 128]
        out[64:128, :] = context[:, i * 256 + 128:(i + 1) * 256]


def here_kernel(count, *refs):
    acc_in, r1, r2, r3, out, acc_s, top_s, kv_s = refs[2 + count:]
    own_sums(refs[0], refs[1], list(refs[2:2 + count]), acc_in, acc_s, top_s, kv_s, 0, 256)
    context = context_of(acc_s[64:128, :], acc_s[0:1, :], top_s[0:1, :], (r1, r2, r3), slice(0, 256))
    out[0:64, :] = context[:, 0:128]
    out[64:128, :] = context[:, 128:256]


def sibling_kernel(c0, c1, c2, c3, out):
    for i, c in enumerate((c0, c1, c2, c3)):
        out[i * 64:(i + 1) * 64, :] = c[64:128, :]


def expand_kernel(pos, c0, c1, c2, c3, theirs, frames, w_out, gain, w_expand, hidden, glu, inner, outer, ctx):
    y, core = pos[0], pos[1]
    for i, c in enumerate((c0, c1, c2, c3)):
        head = lax.rem(y + i, 4)
        ctx[pl.ds(pl.multiple_of((core * 4 + head) * 64, 64), 64), :] = c[0:64, :]
        ctx[pl.ds(pl.multiple_of(((1 - core) * 4 + head) * 64, 64), 64), :] = theirs[i * 64:(i + 1) * 64, :]
    context = ctx[...].T
    h = (frames[...].astype(F32) + mm(context, w_out[...])).astype(BF)
    hidden[...] = h
    normed = norm_rows(h, gain[...]).astype(BF)
    for i in range(2):
        value = mm(normed, w_expand[:, i * 512:(i + 1) * 512])
        gate = mm(normed, w_expand[:, 1024 + i * 512:1024 + (i + 1) * 512])
        g = (value * jax.nn.sigmoid(gate)).astype(BF)
        cols = slice(i * 512, (i + 1) * 512)
        glu[:, cols] = g

    @pl.when(core == 0)
    def _():
        inner[...] = glu[OWN - 16:, :]
        outer[...] = glu[:16, :]

    @pl.when(core == 1)
    def _():
        inner[...] = glu[:16, :]
        outer[...] = glu[OWN - 16:, :]


def conv_kernel(glu, taps, conv, pad):
    for i in range(8):
        pad[i, 0:16, :] = jnp.zeros((16, 128), F32)
        pad[i, 16:16 + OWN, :] = glu[:, i * 128:(i + 1) * 128].astype(F32)
        pad[i, 16 + OWN:32 + OWN, :] = jnp.zeros((16, 128), F32)

    def block(i, carry):
        cols = pl.ds(pl.multiple_of(i * 128, 128), 128)
        total = jnp.zeros((OWN, 128), F32)
        for tap in range(31):
            total = total + taps[tap:tap + 1, cols] * pad[i, 1 + tap:1 + tap + OWN, :]
        conv[:, cols] = total
        return carry

    lax.fori_loop(0, D // 128, block, 0)


def close_kernel(pos, conv, inner, outer, hidden, taps, scale, shift, w_project, out, edge):
    core = pos[1]
    first = jnp.where(core == 0, 1.0, 0.0)
    for i in range(8):
        cols = slice(i * 128, (i + 1) * 128)
        one, two = inner[:, cols].astype(F32), outer[:, cols].astype(F32)
        before = first * two + (1.0 - first) * one
        after = first * one + (1.0 - first) * two
        edge[i, 0:16, :] = before
        edge[i, 16:32, :] = jnp.zeros((16, 128), F32)
        edge[i, 32:48, :] = after
    parts = []
    for i in range(8):
        cols = slice(i * 128, (i + 1) * 128)
        top = conv[0:16, cols]
        low = conv[OWN - 16:OWN, cols]
        for tap in range(15):
            top = top + taps[tap:tap + 1, cols] * edge[i, 1 + tap:17 + tap, :]
            late = 16 + tap
            low = low + taps[late:late + 1, cols] * edge[i, 1 + late:17 + late, :]
        total = jnp.concatenate([top, conv[16:OWN - 16, cols], low], axis=0)
        parts.append(jax.nn.silu(scale[:, cols] * total + shift[:, cols]).astype(BF))
    act = jnp.concatenate(parts, axis=1)
    out[...] = (hidden[...].astype(F32) + mm(act, w_project[...])).astype(BF)


def body(frames, gain_attn, w_query, w_key, w_value, w_out, gain_conv, w_expand, kernel_taps, bn_scale, bn_shift, w_project):
    core = lax.axis_index("core")
    y = lax.axis_index("yhi") * 2 + lax.axis_index("ylo")
    pos = jnp.stack([y, core]).astype(jnp.int32)

    def along(axis, value, step):
        count = lax.axis_size(axis)
        return lax.ppermute(value, axis, [(i, (i + step) % count) for i in range(count)])

    def along_y(value, step):
        place_of = lambda v: v % 2 * 2 + v // 2
        return lax.ppermute(value, ("ylo", "yhi"), [(place_of(i), place_of((i + step) % 4)) for i in range(4)])

    row = lambda v: v.reshape(1, -1)
    stay = lambda v: pltpu.with_memory_space_constraint(v, pltpu.HBM)
    sib = along("core", frames, 1)
    sent = call(
        project_kernel, (pos, stay(frames), sib, stay(row(gain_attn)), stay(w_query), stay(w_key), stay(w_value)),
        [SM, HBM, VM, HBM, HBM, HBM, HBM], [((384, 128), BF)] * 4,
        [pltpu.VMEM((OWN, D), BF), pltpu.VMEM((1, D), F32), pltpu.VMEM((3, D, 256), BF), pltpu.SemaphoreType.DMA((5,))],
    )
    got = [sent[0]] + [along_y(sent[i], i) for i in (1, 2, 3)]
    kv, qx = call(pack_kernel, got, [VM] * 4, [((GRP, 128), BF), ((80, GRP), BF)])
    up1, down1 = along("z", kv, 1), along("z", kv, -1)
    queries = [along("x", qx, i) for i in (1, 2, 3)]
    own_acc, = call(start_kernel, (qx, kv), [VM] * 2, [((72, GRP), F32)], us=2)
    many = ((72, 3 * GRP), F32)
    q_scratch = pltpu.VMEM((80, 3 * GRP), BF)
    acc, = call(
        functools.partial(remote_kernel, 1, True, False), (*queries, kv), [VM] * 4, [many], [q_scratch], us=3,
    )
    up1, down1, own_acc, acc = lax.optimization_barrier((up1, down1, own_acc, acc))
    up2, down2 = along("z", up1, 1), along("z", down1, -1)
    acc, = call(
        functools.partial(remote_kernel, 2, False, False), (*queries, up1, down1, acc), [VM] * 6, [many], [q_scratch], us=7,
    )
    up2, down2, acc = lax.optimization_barrier((up2, down2, acc))
    up3, down3 = along("z", up2, 1), along("z", down2, -1)
    acc, = call(
        functools.partial(remote_kernel, 2, False, False), (*queries, up2, down2, acc), [VM] * 6, [many], [q_scratch], us=7,
    )
    up3, down3, acc = lax.optimization_barrier((up3, down3, acc))
    up4 = along("z", up3, 1)
    acc, = call(
        functools.partial(remote_kernel, 2, False, False), (*queries, up3, down3, acc), [VM] * 6, [many], [q_scratch], us=7,
    )
    parts = call(
        functools.partial(remote_kernel, 1, False, True),
        (*queries, up4, kv, up1, down1, up2, down2, up3, down3, acc), [VM] * 4 + [ANY] * 7 + [VM],
        [((80, GRP), BF)] * 3,
        [q_scratch, pltpu.VMEM((128, 3 * GRP), F32), pltpu.VMEM((8, 3 * GRP), F32), pltpu.VMEM((8, GRP, 128), BF)],
        us=4,
    )
    returned = [along("x", parts[i - 1], -i) for i in (1, 2, 3)]
    chunks = (up1, down1, up2, down2, up3, down3, up4)
    scratch = lambda n: [pltpu.VMEM((128, n), F32), pltpu.VMEM((8, n), F32), pltpu.VMEM((8, GRP, 128), BF)]
    part, = call(
        functools.partial(others_kernel, 7), (qx, kv, *chunks, own_acc), [VM] * 10, [((80, 768), F32)], scratch(768), us=6,
    )
    away = call(combine_kernel, (part, *returned), [VM] * 4, [((128, 128), BF)] * 3, us=1)
    home = [along_y(away[i - 1], -i) for i in (1, 2, 3)]
    here, = call(
        functools.partial(here_kernel, 7), (qx, kv, *chunks, own_acc, *returned), [VM] * 13, [((128, 128), BF)],
        scratch(256), us=3,
    )
    contexts = [here] + home
    theirs, = call(sibling_kernel, contexts, [VM] * 4, [((256, 128), BF)], us=1)
    theirs = along("core", theirs, 1)
    hidden, glu, inner, outer = call(
        expand_kernel, (pos, *contexts, theirs, frames, w_out, row(gain_conv), w_expand), [SM] + [VM] * 9,
        [((OWN, D), BF), ((OWN, D), BF), ((16, D), BF), ((16, D), BF)], [pltpu.VMEM((512, 128), BF)], us=2,
    )
    count = lax.axis_size(NAMES)
    outer = lax.ppermute(
        outer, NAMES, [(i, i - 1) for i in range(2, count, 2)] + [(i, i + 1) for i in range(1, count - 1, 2)]
    )
    inner = along("core", inner, 1)
    conv, = call(conv_kernel, (glu, kernel_taps), [VM] * 2, [((OWN, D), F32)], [pltpu.VMEM((8, OWN + 32, 128), F32)], us=3)
    out, = call(
        close_kernel, (pos, conv, inner, outer, hidden, kernel_taps, row(bn_scale), row(bn_shift), w_project),
        [SM] + [VM] * 8, [((OWN, D), BF)], [pltpu.VMEM((8, 48, 128), F32)], us=2,
    )
    return out


def solution(mesh):
    fine = Mesh(mesh.devices.reshape(2, 8, 4, 2, 2), NAMES)
    rows = P(NAMES, None)
    return jax.shard_map(
        body, mesh=fine, in_specs=(rows,) + (P(),) * 11, out_specs=rows, check_vma=False,
    )
```

```python
import functools

import jax
import jax.numpy as jnp
from jax import lax
from jax.experimental import pallas as pl
from jax.experimental.pallas import tpu as pltpu
from jax.sharding import Mesh
from jax.sharding import PartitionSpec as P

BF = jnp.bfloat16
F32 = jnp.float32
D = 1024
HD = 64
OWN = 128
GRP = 1024
EPS = 1e-05
C = 0.125 * 1.4426950408889634
T_LOW, T_HIGH = 2.0 ** -60, 2.0 ** 100
TQ = 1024
VMEM_LIMIT = 24 * 2 ** 20
NAMES = ("ylo", "z", "x", "yhi", "core")
VM = pl.BlockSpec(memory_space=pltpu.VMEM)
SM = pl.BlockSpec(memory_space=pltpu.SMEM)
ANY = pl.BlockSpec(memory_space=pl.ANY)
HBM = pl.BlockSpec(memory_space=pltpu.HBM)


def call(kernel, ins, specs, outs, scratch=(), us=2):
    return pl.pallas_call(
        kernel,
        in_specs=specs,
        out_specs=[VM] * len(outs),
        out_shape=[jax.ShapeDtypeStruct(s, d) for s, d in outs],
        scratch_shapes=list(scratch),
        compiler_params=pltpu.CompilerParams(vmem_limit_bytes=VMEM_LIMIT),
        cost_estimate=pl.CostEstimate(flops=int(us * 1e9), bytes_accessed=1024, transcendentals=0),
    )(*ins)


def norm_rows(values, gain):
    values = values.astype(F32)
    center = values - jnp.mean(values, axis=-1, keepdims=True)
    spread = jnp.mean(center * center, axis=-1, keepdims=True)
    return center * lax.rsqrt(spread + EPS) * gain


def mm(a, b):
    return jnp.dot(a, b, preferred_element_type=F32)


def split3(row):
    hi = row.astype(BF)
    rest = row - hi.astype(F32)
    mid = rest.astype(BF)
    low = (rest - mid.astype(F32)).astype(BF)
    return hi, mid, low


def stats_rows(total, top):
    width = total.shape[1]
    index = lax.broadcasted_iota(jnp.int32, (16, width), 0)
    out = jnp.zeros((16, width), F32)
    for place, part in enumerate(split3(total) + split3(top)):
        out = jnp.where(index == place, jnp.broadcast_to(part.astype(F32), (16, width)), out)
    return out.astype(BF)


def stats_read(rows):
    rows = rows.astype(F32)
    return rows[0:1] + rows[1:2] + rows[2:3], rows[3:4] + rows[4:5] + rows[5:6]


def fetch_kernel(pos, own_hbm, gain_hbm, wq, wk, wv, w, normed, gain, own, sems):
    cols = pl.ds(pl.multiple_of(pos[1] * 256, 256), 256)
    first = [pltpu.make_async_copy(own_hbm, own, sems.at[3]), pltpu.make_async_copy(gain_hbm, gain, sems.at[4])]
    copies = [pltpu.make_async_copy(v.at[:, cols], w.at[i], sems.at[i]) for i, v in enumerate((wk, wv, wq))]
    for copy in first + copies:
        copy.start()
    for copy in first:
        copy.wait()
    normed[...] = norm_rows(own[...], gain[...]).astype(BF)
    for copy in copies:
        copy.wait()


def project_kernel(pos, own, sib, gain, wbuf, m0, m1, m2, m3):
    y = pos[0]
    normed = jnp.concatenate([own[...], norm_rows(sib[...], gain[...]).astype(BF)], axis=0)
    k = mm(normed, wbuf[0])
    vt = mm(normed, wbuf[1]).T.astype(BF)
    qt = mm(normed, wbuf[2]).T.astype(BF)
    blocks = []
    for h in range(4):
        pair = jnp.concatenate([k[:OWN, h * HD:(h + 1) * HD], k[OWN:, h * HD:(h + 1) * HD]], axis=1).astype(BF)
        vh, qh = vt[h * HD:(h + 1) * HD], qt[h * HD:(h + 1) * HD]
        blocks.append(jnp.concatenate([pair, vh[:, :OWN], vh[:, OWN:], qh[:, :OWN], qh[:, OWN:]], axis=0))
    outs = (m0, m1, m2, m3)
    for here in range(4):
        @pl.when(y == here)
        def _():
            for i in range(4):
                outs[i][...] = blocks[(here + i) % 4]


def pair_and_values(kv, half):
    lhs = kv[0:512, :]
    cols = jnp.concatenate([kv[512 + half * 256 + i * 64:512 + half * 256 + (i + 1) * 64, :] for i in range(4)], axis=1)
    return lhs, jnp.concatenate([jnp.ones((64, 512), BF), cols], axis=0)


def place(q, half):
    zero = jnp.zeros((64, q.shape[1]), BF)
    return jnp.concatenate([q, zero] if half == 0 else [zero, q], axis=0)


def pack_kernel(a0, a1, a2, a3, kv, qx):
    parts = (a0, a1, a2, a3)
    for i, a in enumerate(parts):
        kv[i * 128:(i + 1) * 128, :] = a[0:128, :]
        kv[512 + i * 64:512 + (i + 1) * 64, :] = a[128:192, :]
        kv[768 + i * 64:768 + (i + 1) * 64, :] = a[192:256, :]
        qx[0:64, (2 * i) * 128:(2 * i + 1) * 128] = a[256:320, :]
        qx[0:64, (2 * i + 1) * 128:(2 * i + 2) * 128] = a[320:384, :]
    s = mm(kv[0:512, :], place(qx[0:64, :], 0))
    top = jnp.max(s, axis=0, keepdims=True)
    qx[64:80, :] = stats_rows(jnp.zeros_like(top), top)


def augmented(q, stats):
    unused, top = stats_read(stats)
    shift = top.astype(BF)
    width = shift.shape[1]
    index = lax.broadcasted_iota(jnp.int32, (128, width), 0)
    bias = jnp.where(index == 0, jnp.broadcast_to(-shift.astype(F32), (128, width)), 0.0).astype(BF)
    return [jnp.concatenate([place(q, half), bias], axis=0) for half in (0, 1)], shift.astype(F32)


def one_column(rows):
    lane = lax.broadcasted_iota(jnp.int32, (rows, 128), 1)
    return jnp.where(lane == 0, 1.0, 0.0).astype(BF)


def attend(rhs, chunks, acc):
    ones = one_column(512)

    def weights(step):
        kv, half = chunks[step // 2], step % 2
        lhs, values = pair_and_values(kv, half)
        s = mm(jnp.concatenate([lhs, ones], axis=1), rhs[half])
        return jnp.exp2(s * C).astype(BF), values

    steps = 2 * len(chunks)
    now = weights(0)
    for step in range(steps):
        later = weights(step + 1) if step + 1 < steps else None
        acc = acc + mm(now[1], now[0])
        now = later
    return acc


def exact(q_ref, chunks, kv_s, acc_ref, top_ref, start):
    for i, ref in enumerate(chunks):
        pltpu.sync_copy(ref, kv_s.at[i])

    def tile(t, carry):
        cols = pl.ds(pl.multiple_of(t * 256, 256), 256)
        q = q_ref[0:64, pl.ds(pl.multiple_of(start + t * 256, 256), 256)]

        def chunk(i, state):
            acc, old = state
            kv = kv_s.at[i]
            for half in (0, 1):
                lhs, values = pair_and_values(kv, half)
                s = mm(lhs, place(q, half))
                new = jnp.maximum(old, jnp.max(s, axis=0, keepdims=True))
                p = jnp.exp2((s - new) * C).astype(BF)
                acc = acc * jnp.exp2((old - new) * C) + mm(values, p)
                old = new
            return acc, old

        acc, top = lax.fori_loop(0, 8, chunk, (jnp.zeros((128, 256), F32), jnp.full((1, 256), -jnp.inf, F32)))
        acc_ref[:, cols] = acc
        top_ref[:, cols] = jnp.broadcast_to(top, (8, 256))
        return carry

    lax.fori_loop(0, acc_ref.shape[1] // 256, tile, 0)


def finish(q_ref, chunks, kv_s, acc_ref, top_ref, start=0):
    total = acc_ref[0:1, :]
    fits = jnp.where((total >= T_LOW) & (total <= T_HIGH), 1.0, 0.0)

    @pl.when(jnp.min(fits) < 0.5)
    def _():
        exact(q_ref, chunks, kv_s, acc_ref, top_ref, start)


def tiles_of(q_ref, acc_in, chunks, acc_ref, top_ref, start=0, size=TQ, count=None):
    def tile(t, carry):
        from_cols = pl.ds(pl.multiple_of(start + t * size, 256), size)
        cols = pl.ds(pl.multiple_of(t * size, 256), size)
        rhs, shift = augmented(q_ref[0:64, from_cols], q_ref[64:80, from_cols])
        if acc_in is None:
            acc = jnp.zeros((128, size), F32)
        else:
            rows = acc_in[:, from_cols]
            acc = jnp.concatenate([jnp.broadcast_to(rows[0:1], (56, size)), rows], axis=0)
        acc = attend(rhs, chunks, acc)
        if top_ref is None:
            acc_ref[:, cols] = acc[56:128]
        else:
            acc_ref[:, cols] = acc
            top_ref[:, cols] = jnp.broadcast_to(shift, (8, size))
        return carry

    lax.fori_loop(0, q_ref.shape[1] // size if count is None else count, tile, 0)


def gather_queries(qs, q_s):
    for t in range(3):
        q_s[:, t * GRP:(t + 1) * GRP] = qs[t][...]


def start_kernel(qx, kv, acc):
    tiles_of(qx, None, [kv], acc, None)


def first_kernel(count, *refs):
    acc, q_s = refs[count + 1:]
    for t in range(count):
        q_s[:, t * GRP:(t + 1) * GRP] = refs[t][...]
    tiles_of(q_s, None, [refs[count]], acc, None)


def second_kernel(q1, q2, q3, up, down, acc_near, acc_far, acc, q_s, acc_s):
    gather_queries((q1, q2, q3), q_s)
    acc_s[:, 0:2 * GRP] = acc_near[...]
    acc_s[:, 2 * GRP:3 * GRP] = acc_far[...]
    tiles_of(q_s, acc_s, [up, down], acc, None)


def remote_kernel(count, first, last, *refs):
    refs = list(refs)
    qs, refs = refs[:3], refs[3:]
    chunks, refs = refs[:count], refs[count:]
    before, refs = (refs[:8 - count], refs[8 - count:]) if last else ([], refs)
    acc_in = None
    if not first:
        acc_in, refs = refs[0], refs[1:]
    if not last:
        acc, q_s = refs
        gather_queries(qs, q_s)
        tiles_of(q_s, acc_in, chunks, acc, None)
        return
    out0, out1, out2, q_s, acc_s, top_s, kv_s = refs
    gather_queries(qs, q_s)
    tiles_of(q_s, acc_in, chunks, acc_s, top_s)
    finish(q_s, before + chunks, kv_s, acc_s, top_s)
    for t, out in enumerate((out0, out1, out2)):
        cols = slice(t * GRP, (t + 1) * GRP)
        out[0:64, :] = acc_s[64:128, cols].astype(BF)
        out[64:80, :] = stats_rows(acc_s[0:1, cols], top_s[0:1, cols])


def own_sums(qx, own_kv, chunks, acc_in, acc_s, top_s, kv_s, start, size):
    tiles_of(qx, acc_in, chunks, acc_s, top_s, start, size, 1)
    finish(qx, [own_kv] + chunks, kv_s, acc_s, top_s, start)


def others_kernel(count, *refs):
    acc_in, out, acc_s, top_s, kv_s = refs[2 + count:]
    own_sums(refs[0], refs[1], list(refs[2:2 + count]), acc_in, acc_s, top_s, kv_s, 256, 768)
    out[0:64, :] = acc_s[64:128, :]
    out[64:72, :] = jnp.broadcast_to(acc_s[0:1, :], (8, 768))
    out[72:80, :] = top_s[...]


def context_of(sums, total, top, received, cols):
    sums = [sums] + [r[0:64, cols].astype(F32) for r in received]
    stats = [(total, top)] + [stats_read(r[64:80, cols]) for r in received]
    top = functools.reduce(jnp.maximum, [s[1] for s in stats])
    factors = [jnp.exp2((s[1] - top) * C) for s in stats]
    total = sum(f * s[0] for f, s in zip(factors, stats))
    return (sum(f * s for f, s in zip(factors, sums)) / total).astype(BF)


def combine_kernel(part, r1, r2, r3, c1, c2, c3):
    context = context_of(part[0:64, :], part[64:65, :], part[72:73, :], (r1, r2, r3), slice(256, 1024))
    for i, out in enumerate((c1, c2, c3)):
        out[0:64, :] = context[:, i * 256:i * 256 + 128]
        out[64:128, :] = context[:, i * 256 + 128:(i + 1) * 256]


def here_kernel(count, *refs):
    acc_in, r1, r2, r3, out, acc_s, top_s, kv_s = refs[2 + count:]
    own_sums(refs[0], refs[1], list(refs[2:2 + count]), acc_in, acc_s, top_s, kv_s, 0, 256)
    context = context_of(acc_s[64:128, :], acc_s[0:1, :], top_s[0:1, :], (r1, r2, r3), slice(0, 256))
    out[0:64, :] = context[:, 0:128]
    out[64:128, :] = context[:, 128:256]


def sibling_kernel(c0, c1, c2, c3, out):
    for i, c in enumerate((c0, c1, c2, c3)):
        out[i * 64:(i + 1) * 64, :] = c[64:128, :]


def expand_kernel(pos, c0, c1, c2, c3, theirs, frames, w_out, gain, w_expand, hidden, glu, inner, outer, ctx):
    y, core = pos[0], pos[1]
    for i, c in enumerate((c0, c1, c2, c3)):
        head = lax.rem(y + i, 4)
        ctx[pl.ds(pl.multiple_of((core * 4 + head) * 64, 64), 64), :] = c[0:64, :]
        ctx[pl.ds(pl.multiple_of(((1 - core) * 4 + head) * 64, 64), 64), :] = theirs[i * 64:(i + 1) * 64, :]
    context = ctx[...].T
    h = (frames[...].astype(F32) + mm(context, w_out[...])).astype(BF)
    hidden[...] = h
    normed = norm_rows(h, gain[...]).astype(BF)
    for i in range(2):
        value = mm(normed, w_expand[:, i * 512:(i + 1) * 512])
        gate = mm(normed, w_expand[:, 1024 + i * 512:1024 + (i + 1) * 512])
        g = (value * jax.nn.sigmoid(gate)).astype(BF)
        cols = slice(i * 512, (i + 1) * 512)
        glu[:, cols] = g

    @pl.when(core == 0)
    def _():
        inner[...] = glu[OWN - 16:, :]
        outer[...] = glu[:16, :]

    @pl.when(core == 1)
    def _():
        inner[...] = glu[:16, :]
        outer[...] = glu[OWN - 16:, :]


def conv_kernel(glu, taps, conv, pad):
    for i in range(8):
        pad[i, 0:16, :] = jnp.zeros((16, 128), F32)
        pad[i, 16:16 + OWN, :] = glu[:, i * 128:(i + 1) * 128].astype(F32)
        pad[i, 16 + OWN:32 + OWN, :] = jnp.zeros((16, 128), F32)

    def block(i, carry):
        cols = pl.ds(pl.multiple_of(i * 128, 128), 128)
        total = jnp.zeros((OWN, 128), F32)
        for tap in range(31):
            total = total + taps[tap:tap + 1, cols] * pad[i, 1 + tap:1 + tap + OWN, :]
        conv[:, cols] = total
        return carry

    lax.fori_loop(0, D // 128, block, 0)


def close_kernel(pos, conv, inner, outer, hidden, taps, scale, shift, w_project, out, edge):
    core = pos[1]
    first = jnp.where(core == 0, 1.0, 0.0)
    for i in range(8):
        cols = slice(i * 128, (i + 1) * 128)
        one, two = inner[:, cols].astype(F32), outer[:, cols].astype(F32)
        before = first * two + (1.0 - first) * one
        after = first * one + (1.0 - first) * two
        edge[i, 0:16, :] = before
        edge[i, 16:32, :] = jnp.zeros((16, 128), F32)
        edge[i, 32:48, :] = after
    parts = []
    for i in range(8):
        cols = slice(i * 128, (i + 1) * 128)
        top = conv[0:16, cols]
        low = conv[OWN - 16:OWN, cols]
        for tap in range(15):
            top = top + taps[tap:tap + 1, cols] * edge[i, 1 + tap:17 + tap, :]
            late = 16 + tap
            low = low + taps[late:late + 1, cols] * edge[i, 1 + late:17 + late, :]
        total = jnp.concatenate([top, conv[16:OWN - 16, cols], low], axis=0)
        parts.append(jax.nn.silu(scale[:, cols] * total + shift[:, cols]).astype(BF))
    act = jnp.concatenate(parts, axis=1)
    out[...] = (hidden[...].astype(F32) + mm(act, w_project[...])).astype(BF)


def body(frames, gain_attn, w_query, w_key, w_value, w_out, gain_conv, w_expand, kernel_taps, bn_scale, bn_shift, w_project):
    core = lax.axis_index("core")
    y = lax.axis_index("yhi") * 2 + lax.axis_index("ylo")
    pos = jnp.stack([y, core]).astype(jnp.int32)

    def along(axis, value, step):
        count = lax.axis_size(axis)
        return lax.ppermute(value, axis, [(i, (i + step) % count) for i in range(count)])

    def along_y(value, step):
        place_of = lambda v: v % 2 * 2 + v // 2
        return lax.ppermute(value, ("ylo", "yhi"), [(place_of(i), place_of((i + step) % 4)) for i in range(4)])

    row = lambda v: v.reshape(1, -1)
    stay = lambda v: pltpu.with_memory_space_constraint(v, pltpu.HBM)
    sib = along("core", frames, 1)
    weights, normed, gain = call(
        fetch_kernel, (pos, stay(frames), stay(row(gain_attn)), stay(w_query), stay(w_key), stay(w_value)),
        [SM, HBM, HBM, HBM, HBM, HBM], [((3, D, 256), BF), ((OWN, D), BF), ((1, D), F32)],
        [pltpu.VMEM((OWN, D), BF), pltpu.SemaphoreType.DMA((5,))], us=2,
    )
    sent = call(project_kernel, (pos, normed, sib, gain, weights), [SM] + [VM] * 4, [((384, 128), BF)] * 4)
    got = [sent[0]] + [along_y(sent[i], i) for i in (1, 2, 3)]
    kv, qx = call(pack_kernel, got, [VM] * 4, [((GRP, 128), BF), ((80, GRP), BF)])
    up1, down1 = along("z", kv, 1), along("z", kv, -1)
    queries = [along("x", qx, i) for i in (1, 2, 3)]
    own_acc, = call(start_kernel, (qx, kv), [VM] * 2, [((72, GRP), F32)], us=2)
    many = ((72, 3 * GRP), F32)
    q_scratch = pltpu.VMEM((80, 3 * GRP), BF)
    order = (1, 3, 2)
    queries = [queries[i - 1] for i in order]
    acc_near, = call(
        functools.partial(first_kernel, 2), (*queries[:2], kv), [VM] * 3, [((72, 2 * GRP), F32)],
        [pltpu.VMEM((80, 2 * GRP), BF)], us=2,
    )
    acc_far, = call(
        functools.partial(first_kernel, 1), (queries[2], kv), [VM] * 2, [((72, GRP), F32)], [pltpu.VMEM((80, GRP), BF)], us=1,
    )
    up1, down1, own_acc, acc_near, acc_far = lax.optimization_barrier((up1, down1, own_acc, acc_near, acc_far))
    up2, down2 = along("z", up1, 1), along("z", down1, -1)
    acc, = call(
        second_kernel, (*queries, up1, down1, acc_near, acc_far), [VM] * 7, [many],
        [q_scratch, pltpu.VMEM((72, 3 * GRP), F32)], us=7,
    )
    up2, down2, acc = lax.optimization_barrier((up2, down2, acc))
    up3, down3 = along("z", up2, 1), along("z", down2, -1)
    acc, = call(
        functools.partial(remote_kernel, 2, False, False), (*queries, up2, down2, acc), [VM] * 6, [many], [q_scratch], us=7,
    )
    up3, down3, acc = lax.optimization_barrier((up3, down3, acc))
    up4 = along("z", up3, 1)
    acc, = call(
        functools.partial(remote_kernel, 2, False, False), (*queries, up3, down3, acc), [VM] * 6, [many], [q_scratch], us=7,
    )
    parts = call(
        functools.partial(remote_kernel, 1, False, True),
        (*queries, up4, kv, up1, down1, up2, down2, up3, down3, acc), [VM] * 4 + [ANY] * 7 + [VM],
        [((80, GRP), BF)] * 3,
        [q_scratch, pltpu.VMEM((128, 3 * GRP), F32), pltpu.VMEM((8, 3 * GRP), F32), pltpu.VMEM((8, GRP, 128), BF)],
        us=4,
    )
    returned = [along("x", part, -i) for i, part in zip(order, parts)]
    chunks = (up1, down1, up2, down2, up3, down3, up4)
    scratch = lambda n: [pltpu.VMEM((128, n), F32), pltpu.VMEM((8, n), F32), pltpu.VMEM((8, GRP, 128), BF)]
    part, = call(
        functools.partial(others_kernel, 7), (qx, kv, *chunks, own_acc), [VM] * 10, [((80, 768), F32)], scratch(768), us=6,
    )
    away = call(combine_kernel, (part, *returned), [VM] * 4, [((128, 128), BF)] * 3, us=1)
    home = [along_y(away[i - 1], -i) for i in (1, 2, 3)]
    here, = call(
        functools.partial(here_kernel, 7), (qx, kv, *chunks, own_acc, *returned), [VM] * 13, [((128, 128), BF)],
        scratch(256), us=3,
    )
    contexts = [here] + home
    theirs, = call(sibling_kernel, contexts, [VM] * 4, [((256, 128), BF)], us=1)
    theirs = along("core", theirs, 1)
    hidden, glu, inner, outer = call(
        expand_kernel, (pos, *contexts, theirs, frames, w_out, row(gain_conv), w_expand), [SM] + [VM] * 9,
        [((OWN, D), BF), ((OWN, D), BF), ((16, D), BF), ((16, D), BF)], [pltpu.VMEM((512, 128), BF)], us=2,
    )
    count = lax.axis_size(NAMES)
    outer = lax.ppermute(
        outer, NAMES, [(i, i - 1) for i in range(2, count, 2)] + [(i, i + 1) for i in range(1, count - 1, 2)]
    )
    conv, = call(conv_kernel, (glu, kernel_taps), [VM] * 2, [((OWN, D), F32)], [pltpu.VMEM((8, OWN + 32, 128), F32)], us=3)
    inner, conv = lax.optimization_barrier((inner, conv))
    inner = along("core", inner, 1)
    out, = call(
        close_kernel, (pos, conv, inner, outer, hidden, kernel_taps, row(bn_scale), row(bn_shift), w_project),
        [SM] + [VM] * 8, [((OWN, D), BF)], [pltpu.VMEM((8, 48, 128), F32)], us=2,
    )
    return out


def solution(mesh):
    fine = Mesh(mesh.devices.reshape(2, 8, 4, 2, 2), NAMES)
    rows = P(NAMES, None)
    return jax.shard_map(
        body, mesh=fine, in_specs=(rows,) + (P(),) * 11, out_specs=rows, check_vma=False,
    )
```
